32 devices in a mesh: groups: 2 (over y), seq: 4 (over z), clus: 2 (over x), dp: 2 (over core).
Axes of the slice: x: 2, y: 2, z: 4, core: 2. Of those that a mesh axis runs over, the one named last changes fastest.
Arguments:
- layer_input: bfloat16 [4, 2048, 2048], P(('groups', 'dp'), 'seq'), parts along dimension 0, may hold values from -6 to 6
- queries: bfloat16 [4, 2048, 1024], P(('groups', 'dp'), 'seq', 'clus'), parts along dimension 0, may hold values from -18 to 18
- keys: bfloat16 [4, 2048, 1024], P(('groups', 'dp'), 'seq', 'clus'), parts along dimension 0, may hold values from -18 to 18
- values: bfloat16 [4, 2048, 1024], P(('groups', 'dp'), 'seq', 'clus'), parts along dimension 0, may hold values from -6 to 6
- out_grad: bfloat16 [4, 2048, 1024], P(('groups', 'dp'), 'seq', 'clus'), parts along dimension 0, may hold values from -6 to 6
- cluster_ids: int32 [4, 8, 2048], P(('groups', 'dp'), 'clus', 'seq'), parts along dimension 0, may hold values from 0 to 3
- slots: int32 [4, 8, 2048], P(('groups', 'dp'), 'clus', 'seq'), parts along dimension 0, may hold values from -1 to 1023, as said below
- counts: int32 [4, 8, 4, 4], P(('groups', 'dp'), 'clus', 'seq'), parts along dimension 0, may hold values from 0 to 256, as said below
Outputs:
- query_grad: bfloat16 [4, 2048, 1024], P(('groups', 'dp'), 'seq', 'clus'), parts along dimension 0
- key_grad: bfloat16 [4, 2048, 1024], P(('groups', 'dp'), 'seq', 'clus'), parts along dimension 0
- value_grad: bfloat16 [4, 2048, 1024], P(('groups', 'dp'), 'seq', 'clus'), parts along dimension 0
- weight_grad: float32 [4096, 3, 1024], P(('groups', 'seq'), None, 'clus'), parts along dimension 0
- centroid_dirs: float32 [16, 4, 128], P(('groups', 'clus'), 'seq'), parts along dimension 0
The draws below stay inside these ranges and needn't reach their ends.
There are 2 independent parts, one for each index of `groups`. The reference program is written for one: setup_inputs(seed, part) draws one part's arguments, and reference() takes and returns one part's arrays. A program takes and returns all parts, laid end to end along the dimension named above; each array names one. Nothing has to cross between parts.
Inputs may be any that keep to these rules, and one draw needn't show every extreme that they name: `slots`: -1 marks a token left out of its cluster; otherwise the slot is s * 256 + r, where s is the index along seq of the device that holds the token and r counts the earlier kept tokens of that device with the same cluster and head, so at most 256 tokens of one device are kept in one cluster; in every head of every clip some cluster keeps 256 tokens from every device. counts[b, h, j, s] is the number of tokens of device s kept in cluster j of head h, the same as given by slots.
All inputs are finite; a program needn't handle non-finite values.
Results may differ from the reference program's by a relative error of at most 0.012.
The reference program's roundings to bfloat16 on the way count: a program that leaves them out, or rounds other values in their place, can miss the bound.
Values may be sent and summed in bfloat16 or wider, within the bound.
A program may use at most 64 MiB of HBM per device.

```python
import jax
import jax.numpy as jnp
from jax import lax

D = 2048
E = 128
HEADS = 8
CAP = 1024
HE = 1024
CLIPS = 2
SOURCES = 4
SEND = 256
NCL = 4
TOK_DEV = 512
SEQLEN = 2048


def routing(key):
    key = jax.random.fold_in(key, 101)
    hot_key, pick_key, order_key = jax.random.split(key, 3)
    hot = jax.random.randint(hot_key, (CLIPS, HEADS, 1, 1), 0, NCL)
    picked = jax.random.randint(pick_key, (CLIPS, HEADS, SOURCES, TOK_DEV), 0, NCL)
    noise = jax.random.randint(order_key, (CLIPS, HEADS, SOURCES, TOK_DEV), 0, 2 ** 18)
    distinct = noise * TOK_DEV + jnp.arange(TOK_DEV, dtype=jnp.int32)
    order = jnp.argsort(distinct, axis=-1)
    ranks = jnp.argsort(order, axis=-1)
    chosen = jnp.where(ranks < SEND, hot, picked).astype(jnp.int32)
    member = (chosen[..., None] == jnp.arange(NCL, dtype=jnp.int32)).astype(jnp.int32)
    before = jnp.cumsum(member, axis=3) - member
    place = jnp.sum(before * member, axis=-1)
    source = jnp.arange(SOURCES, dtype=jnp.int32)[:, None]
    slot = jnp.where(place < SEND, source * SEND + place, -1).astype(jnp.int32)
    tally = jnp.minimum(jnp.sum(member, axis=3), SEND).astype(jnp.int32)
    tally = jnp.transpose(tally, (0, 1, 3, 2))
    return (chosen.reshape(CLIPS, HEADS, SEQLEN), slot.reshape(CLIPS, HEADS, SEQLEN), tally)


def log_spread(key, shape, low, high):
    return jnp.exp(jax.random.uniform(key, shape, jnp.float32, jnp.log(low), jnp.log(high)))


def draw_cluster_ids(key, part):
    return routing(key)[0]


def draw_slots(key, part):
    return routing(key)[1]


def draw_counts(key, part):
    return routing(key)[2]


def draw_queries(key, part):
    key = jax.random.fold_in(key, 3)
    first = jax.random.fold_in(key, 0)
    third = jax.random.fold_in(key, 2)
    fourth = jax.random.fold_in(key, 3)
    shape = (CLIPS, SEQLEN, HEADS, E)
    columns = log_spread(third, (HEADS, E), 0.3, 3.0)
    base = jax.random.truncated_normal(fourth, -3.0, 3.0, shape, jnp.float32)
    rows = log_spread(first, (CLIPS, SEQLEN, HEADS, 1), 0.5, 2.0)
    result = base * columns * rows
    return result.reshape(CLIPS, SEQLEN, HE).astype(jnp.bfloat16)


def draw_keys(key, part):
    key = jax.random.fold_in(key, 4)
    first, third, fourth = jax.random.split(key, 3)
    shape = (CLIPS, SEQLEN, HEADS, E)
    columns = log_spread(third, (HEADS, E), 0.3, 3.0)
    base = jax.random.truncated_normal(fourth, -3.0, 3.0, shape, jnp.float32)
    rows = log_spread(first, (CLIPS, SEQLEN, HEADS, 1), 0.5, 2.0)
    result = base * columns * rows
    return result.reshape(CLIPS, SEQLEN, HE).astype(jnp.bfloat16)


def levels(stream_key, extent, pieces, least, high):
    factor_of, own = 1.0, jax.random.fold_in(stream_key, 6)
    for dim, blocks in pieces:
        steps = jnp.exp(jax.random.uniform(jax.random.fold_in(own, dim), (blocks,), jnp.float32, least / len(pieces), high / len(pieces)))
        factor_of = factor_of * jnp.repeat(steps, extent[dim] // blocks).reshape([-1 if axis == dim else 1 for axis in range(len(extent))])
    return factor_of


def gaussian(own_key, shape, spread, limit, shards=(), kind=jnp.bfloat16):
    level = levels(own_key, shape, shards, -0.22, 0.18) if shards else 1.0
    values = jax.random.normal(own_key, shape, jnp.float32) * spread * level
    return jnp.minimum(jnp.maximum(values, -limit), limit).astype(kind)


def setup_inputs(seed: int = 0, part: int = 0) -> dict:
    streams_of = jax.random.split(jax.random.key(seed), 9)
    own_keys = jax.random.split(jax.random.fold_in(streams_of[8], part), 9)
    layer_input = gaussian(own_keys[0], (CLIPS, SEQLEN, D), 1.0, 6.0, ((0, 2), (1, 4)))
    queries = draw_queries(jax.random.fold_in(jax.random.fold_in(streams_of[8], part), 71), part)
    keys = draw_keys(jax.random.fold_in(jax.random.fold_in(streams_of[8], part), 71), part)
    values = gaussian(own_keys[3], (CLIPS, SEQLEN, HE), 1.0, 6.0, ((0, 2), (1, 4), (2, 2)))
    out_grad = gaussian(own_keys[4], (CLIPS, SEQLEN, HE), 1.0, 6.0, ((0, 2), (1, 4), (2, 2)))
    cluster_ids = draw_cluster_ids(jax.random.fold_in(jax.random.fold_in(streams_of[8], part), 71), part)
    slots = draw_slots(jax.random.fold_in(jax.random.fold_in(streams_of[8], part), 71), part)
    counts = draw_counts(jax.random.fold_in(jax.random.fold_in(streams_of[8], part), 71), part)
    return {"layer_input": layer_input, "queries": queries, "keys": keys, "values": values, "out_grad": out_grad, "cluster_ids": cluster_ids, "slots": slots, "counts": counts}


def contract_rows(left, right):
    return lax.dot_general(left, right, (((0,), (0,)), ((), ())), preferred_element_type=jnp.float32)

def contract_cols(left, right):
    return lax.dot_general(left, right, (((1,), (1,)), ((), ())), preferred_element_type=jnp.float32)

def unit_rows(array):
    wide = array.astype(jnp.float32)
    return wide * lax.rsqrt(lax.optimization_barrier(jnp.mean(wide * wide, axis=-1, keepdims=True)) + 1e-06)

def block_backward(block, live, rows):
    width = block.shape[1] // 4
    scale = width ** (-0.5)
    query = block[:, :width]
    key = block[:, width:2 * width]
    value = block[:, 2 * width:3 * width]
    grad = block[:, 3 * width:]
    key_total = jnp.zeros((block.shape[0], width), jnp.float32)
    value_total = jnp.zeros((block.shape[0], width), jnp.float32)
    query_parts = []
    for start in range(0, block.shape[0], rows):
        query_rows = query[start:start + rows]
        grad_rows = grad[start:start + rows]
        scores = contract_cols(query_rows, key) * scale
        scores = jnp.where(live[None, :], scores, -1e+30)
        top = lax.optimization_barrier(jnp.max(scores, axis=1, keepdims=True))
        weights = jnp.exp(scores - top)
        probs = weights / lax.optimization_barrier(jnp.sum(weights, axis=1, keepdims=True))
        probs_low = probs.astype(jnp.bfloat16)
        recomputed = jnp.dot(probs_low, value, preferred_element_type=jnp.float32)
        delta = lax.optimization_barrier(jnp.sum(grad_rows.astype(jnp.float32) * recomputed, axis=1, keepdims=True))
        dprobs = contract_cols(grad_rows, value)
        dscores = (probs * (dprobs - delta)).astype(jnp.bfloat16)
        query_parts.append(jnp.dot(dscores, key, preferred_element_type=jnp.float32) * scale)
        key_total = key_total + contract_rows(dscores, query_rows)
        value_total = value_total + contract_rows(probs_low, grad_rows)
    query_total = jnp.concatenate(query_parts, axis=0)
    return jnp.concatenate((query_total, key_total * scale, value_total), axis=1).astype(jnp.bfloat16)

def head_pass(query, key, value, grad, cluster, slot, count):
    kept = slot >= 0
    place = jnp.where(kept, cluster * CAP + slot, NCL * CAP).astype(jnp.int32)
    rows = jnp.concatenate((query, key, value, grad), axis=1)
    blocks = jnp.zeros((NCL * CAP + 1, rows.shape[1]), rows.dtype).at[place].set(rows)
    blocks = blocks[:NCL * CAP].reshape(NCL, CAP, rows.shape[1])
    within = jnp.arange(CAP, dtype=jnp.int32)
    live = (within % SEND)[None, :] < count[:, within // SEND]
    grads = lax.map(lambda item: block_backward(item[0], item[1], min(CAP, 512)), (blocks, live))
    flat = jnp.concatenate((grads.reshape(NCL * CAP, grads.shape[2]), jnp.zeros((1, grads.shape[2]), grads.dtype)), axis=0)
    back = flat[place]
    unit = (unit_rows(query) + unit_rows(key)) * kept[:, None].astype(jnp.float32)
    sums = jax.ops.segment_sum(unit, cluster, num_segments=NCL)
    return (back, sums)

def reference(layer_input, queries, keys, values, out_grad, cluster_ids, slots, counts):
    query_list, key_list, value_list = ([], [], [])
    weight_total = jnp.zeros((D, 3 * HE), jnp.float32)
    centroid_total = jnp.zeros((HEADS, NCL, E), jnp.float32)
    for clip in range(CLIPS):

        def split(array):
            return array[clip].reshape(SEQLEN, HEADS, E).transpose(1, 0, 2)
        back, sums = lax.map(lambda item: head_pass(*item), (split(queries), split(keys), split(values), split(out_grad), cluster_ids[clip], slots[clip], counts[clip]))

        def token_major(part):
            return part.transpose(1, 0, 2).reshape(SEQLEN, HE)
        query_grad = token_major(back[:, :, :E])
        key_grad = token_major(back[:, :, E:2 * E])
        value_grad = token_major(back[:, :, 2 * E:])
        query_list.append(query_grad)
        key_list.append(key_grad)
        value_list.append(value_grad)
        stacked = jnp.stack((query_grad, key_grad, value_grad), axis=1).reshape(SOURCES, TOK_DEV, 3 * HE)
        inputs = layer_input[clip].reshape(SOURCES, TOK_DEV, D)

        def add_term(total, item):
            term = contract_rows(item[0], item[1])
            low = lax.optimization_barrier(term.astype(jnp.bfloat16))
            return (total + low.astype(jnp.float32), None)
        clip_total, _ = lax.scan(add_term, jnp.zeros((D, 3 * HE), jnp.float32), (inputs, stacked))
        weight_total = weight_total + clip_total
        centroid_total = centroid_total + sums
    weight_grad = weight_total.reshape(D, 3, HE)
    centroid_dirs = centroid_total * lax.rsqrt(lax.optimization_barrier(jnp.mean(centroid_total * centroid_total, axis=-1, keepdims=True)) + 1e-06)
    return (jnp.stack(query_list), jnp.stack(key_list), jnp.stack(value_list), weight_grad, centroid_dirs)
```

```python
import functools

import jax
import jax.numpy as jnp
from jax import lax
from jax.experimental import pallas as pl
from jax.experimental.pallas import tpu as pltpu
from jax.sharding import PartitionSpec as P

CAP = 1024
MESH = pl.DeviceIdType.MESH
LOG2E = 1.4426950408889634
FAR = 131072.0


def dot(left, right, left_dim, right_dim):
    return lax.dot_general(
        left, right, (((left_dim,), (right_dim,)), ((), ())), preferred_element_type=jnp.float32
    )


def exchange(
    sources, tokens, width, model, clusters,
    layer, queries, keys, values, grads, ids,
    query_out, key_out, value_out, weight_out, dirs_out,
    rows, ids_all, query_wide, key_wide, keep, probs, key_sum, value_sum, back, landed,
    layer_rows, layer_cols, sib_term, sib_in, term, from_left, from_right, total,
    cent_mine, cent_sib, cent_all,
    row_send, row_recv, id_send, id_recv, local_sem, back_send, back_recv,
    sib_send, sib_recv, hop_send, left_recv, right_recv, half_send, half_recv,
    cent_send, cent_recv, out_sem,
):
    me = lax.axis_index("seq")
    core = lax.axis_index("dp")
    other = 1 - core
    scale = width ** (-0.5)
    peers = [lax.rem(me + step, sources) for step in range(1, sources)]
    my_rows = pl.ds(pl.multiple_of(me * tokens, tokens), tokens)
    my_cols = pl.ds(pl.multiple_of(me * width, width), width)
    stream = (queries, keys, values, grads)
    half = model // sources // 2
    every = sources * tokens

    layer_in = pltpu.make_async_copy(layer, layer_rows, out_sem.at[0])
    layer_in.start()
    barrier = pltpu.get_barrier_semaphore()
    for peer in peers:
        pl.semaphore_signal(barrier, inc=1, device_id={"seq": peer}, device_id_type=MESH)
    pl.semaphore_signal(barrier, inc=1, device_id={"dp": other}, device_id_type=MESH)
    pl.semaphore_wait(barrier, sources)

    def remote(src, dst, send, recv, target):
        copy = pltpu.make_async_remote_copy(
            src_ref=src, dst_ref=dst, send_sem=send, recv_sem=recv,
            device_id=target, device_id_type=MESH,
        )
        copy.start()
        return copy

    id_copies = [
        remote(ids.at[peer], ids_all.at[me], id_send.at[n], id_recv.at[n], {"seq": peer})
        for n, peer in enumerate(peers)
    ]
    row_copies = []
    for t in range(4):
        copies = []
        for n, peer in enumerate(peers):
            cols = pl.ds(pl.multiple_of(peer * width, width), width)
            copies.append(
                remote(
                    stream[t].at[:, cols], rows.at[t, my_rows, :],
                    row_send.at[t, n], row_recv.at[t, n], {"seq": peer},
                )
            )
        row_copies.append(copies)
    local = [
        pltpu.make_async_copy(stream[t].at[:, my_cols], rows.at[t, my_rows, :], local_sem.at[t])
        for t in range(4)
    ]
    local.append(pltpu.make_async_copy(ids.at[me], ids_all.at[me], local_sem.at[4]))
    for copy in local:
        copy.start()

    layer_in.wait()
    piece = 256

    def turn(n, carry):
        cols = pl.ds(pl.multiple_of(n * piece, piece), piece)
        layer_cols[cols, :] = layer_rows[:, cols].T
        return carry

    lax.fori_loop(0, model // piece, turn, 0)

    local[4].wait()
    for copy in id_copies:
        copy.wait()
    lane = lax.broadcasted_iota(jnp.int32, (128, 128), 1)
    sub = lax.broadcasted_iota(jnp.int32, (128, 128), 0)
    eye = jnp.where(lane == sub, 1.0, 0.0).astype(jnp.bfloat16)
    inside = jnp.where(sub < clusters, 1.0, 0.0).astype(jnp.bfloat16)
    level = lax.broadcasted_iota(jnp.int32, (128, tokens), 0).astype(jnp.float32)

    for t in range(2):
        local[t].wait()
        for copy in row_copies[t]:
            copy.wait()

    def unit(array):
        wide = array.astype(jnp.float32)
        return wide * lax.rsqrt(jnp.mean(wide * wide, axis=-1, keepdims=True) + 1e-06)

    cent = jnp.zeros((128, width), jnp.float32)
    for s in range(sources):
        span = slice(s * tokens, (s + 1) * tokens)
        member = jnp.where(level == ids_all[s, 0:1, :], 1.0, 0.0).astype(jnp.bfloat16)
        column = dot(member, eye, 0, 0)
        keep[span, :] = dot(member, inside, 0, 0)
        query_wide[span, :width] = rows[0, span, :]
        key_wide[span, :width] = rows[1, span, :]
        query_wide[span, width:] = column.astype(jnp.bfloat16)
        key_wide[span, width:] = ((column - 1.0) * FAR).astype(jnp.bfloat16)
        both = unit(rows[0, span, :]) + unit(rows[1, span, :])
        high = both.astype(jnp.bfloat16)
        low = (both - high.astype(jnp.float32)).astype(jnp.bfloat16)
        cent = cent + dot(member, high, 1, 0) + dot(member, low, 1, 0)
    cent_mine[...] = cent[: cent_mine.shape[0], :]
    cent_first = remote(cent_mine, cent_sib, cent_send.at[0], cent_recv.at[0], {"dp": other})

    chunk = probs.shape[2]
    chunks = every // chunk

    def soft(n, carry):
        span = pl.ds(pl.multiple_of(n * chunk, chunk), chunk)
        scores = dot(key_wide[...], query_wide[span, :], 1, 1)
        top = jnp.max(scores, axis=0, keepdims=True)
        weights = jnp.exp2((scores - top) * (scale * LOG2E))
        probs[n] = weights * (1.0 / jnp.sum(weights, axis=0, keepdims=True))
        return carry

    lax.fori_loop(0, chunks, soft, 0)

    cent_first.wait()
    cent_all[me] = cent_mine[...] + cent_sib[...]
    cent_copies = [
        remote(
            cent_all.at[me], cent_all.at[me], cent_send.at[n + 1], cent_recv.at[n + 1],
            {"seq": peer},
        )
        for n, peer in enumerate(peers)
    ]
    for t in range(2, 4):
        local[t].wait()
        for copy in row_copies[t]:
            copy.wait()
    key_sum[...] = jnp.zeros_like(key_sum)
    value_sum[...] = jnp.zeros_like(value_sum)

    def backward(n, carry):
        span = pl.ds(pl.multiple_of(n * chunk, chunk), chunk)
        query = rows[0, span, :]
        grad = rows[3, span, :]
        share = probs[n]
        share_low = share.astype(jnp.bfloat16)
        dprobs = dot(rows[2], grad, 1, 1)
        delta = jnp.sum(share_low.astype(jnp.float32) * dprobs, axis=0, keepdims=True)
        dscores = (share * (dprobs - delta)).astype(jnp.bfloat16)
        value_sum[...] += dot(share_low, grad, 1, 0)
        key_sum[...] += dot(dscores, query, 1, 0)
        query_part = dot(dscores, rows[1], 0, 0)
        back[0, span, :] = (query_part * (keep[span, :] * scale)).astype(jnp.bfloat16)
        return carry

    lax.fori_loop(0, chunks, backward, 0)
    back[1] = (key_sum[...] * (keep[...] * scale)).astype(jnp.bfloat16)
    back[2] = (value_sum[...] * keep[...]).astype(jnp.bfloat16)

    back_copies = []
    for t in range(3):
        copies = []
        for n, peer in enumerate(peers):
            span = pl.ds(pl.multiple_of(peer * tokens, tokens), tokens)
            copies.append(
                remote(
                    back.at[t, span, :], landed.at[t, :, my_cols],
                    back_send.at[t, n], back_recv.at[t, n], {"seq": peer},
                )
            )
        back_copies.append(copies)
        landed[t, :, my_cols] = back[t, my_rows, :]

    outs = []
    for t, out in enumerate((query_out, key_out, value_out)):
        for copy in back_copies[t]:
            copy.wait()
        outs.append(pltpu.make_async_copy(landed.at[t], out, out_sem.at[t + 1]))
        outs[-1].start()

    def part(d, side, t):
        span = pl.ds(pl.multiple_of(d * (2 * half) + side * half, half), half)
        return dot(layer_cols[span, :], landed[t], 1, 0).astype(jnp.bfloat16)

    low_first = jnp.where(me < sources // 2, 1, 0)
    order = []
    for k in range(sources // 2):
        order.append(jnp.where(low_first == 1, sources - 1 - k, k))
        order.append(jnp.where(low_first == 1, k, sources - 1 - k))

    sib_copies = []
    for d in order:
        for t in range(3):
            sib_term[d, t] = part(d, other, t)
        sib_copies.append(
            remote(sib_term.at[d], sib_in.at[d], sib_send.at[d], sib_recv.at[d], {"dp": other})
        )
    for d in order:
        for t in range(3):
            term[d, t] = part(d, core, t)

    def add(d, arrived):
        for t in range(3):
            term[d, t] = (
                term[d, t].astype(jnp.float32) + arrived[d, t].astype(jnp.float32)
            ).astype(jnp.bfloat16)

    def hop(d, side):
        if side > 0:
            return pltpu.make_async_remote_copy(
                src_ref=term.at[d], dst_ref=from_left.at[d], send_sem=hop_send.at[d],
                recv_sem=left_recv.at[d], device_id={"seq": me + 1}, device_id_type=MESH,
            )
        return pltpu.make_async_remote_copy(
            src_ref=term.at[d], dst_ref=from_right.at[d], send_sem=hop_send.at[d],
            recv_sem=right_recv.at[d], device_id={"seq": me - 1}, device_id_type=MESH,
        )

    last = sources - 1
    for k, d in enumerate(order):
        sib_copies[k].wait_recv()
        add(d, sib_in)

        @pl.when(jnp.logical_and(me < d, me > 0))
        def _():
            hop(d, 1).wait_recv()
            add(d, from_left)

        @pl.when(jnp.logical_and(me > d, me < last))
        def _():
            hop(d, -1).wait_recv()
            add(d, from_right)

        @pl.when(me < d)
        def _():
            hop(d, 1).start()

        @pl.when(me > d)
        def _():
            hop(d, -1).start()

    for t in range(3):
        total[core, t] = term[me, t].astype(jnp.float32)

    @pl.when(me > 0)
    def _():
        hop(me, 1).wait_recv()
        for t in range(3):
            total[core, t] += from_left[me, t].astype(jnp.float32)

    @pl.when(me < last)
    def _():
        hop(me, -1).wait_recv()
        for t in range(3):
            total[core, t] += from_right[me, t].astype(jnp.float32)

    final = remote(total.at[core], total.at[core], half_send, half_recv, {"dp": other})
    for copy in cent_copies:
        copy.wait()
    sums = [cent_all[h, pl.ds(me, 1), :] for h in range(sources)]
    sums = jnp.concatenate(sums, axis=0)
    dirs_out[...] = sums * lax.rsqrt(jnp.mean(sums * sums, axis=-1, keepdims=True) + 1e-06)
    for k, d in enumerate(order):
        sib_copies[k].wait_send()

        @pl.when(me < d)
        def _():
            hop(d, 1).wait_send()

        @pl.when(me > d)
        def _():
            hop(d, -1).wait_send()

    def store(side, sem):
        for t in range(3):
            copy = pltpu.make_async_copy(
                total.at[side, t],
                weight_out.at[t, pl.ds(pl.multiple_of(side * half, half), half), :],
                out_sem.at[sem + t],
            )
            copy.start()
            outs.append(copy)

    store(core, 4)
    final.wait()
    store(other, 7)
    for copy in outs:
        copy.wait()


def by_head(layer_input, queries, keys, values, out_grad, cluster_ids, slots, counts):
    sources = lax.axis_size("seq")
    heads_here = cluster_ids.shape[1]
    tokens = queries.shape[1]
    width = queries.shape[2] // heads_here
    model = layer_input.shape[2]
    clusters = sources * counts.shape[2]
    every = sources * tokens
    half = model // sources // 2
    cols = heads_here * width
    chunk = 256
    low, wide = jnp.bfloat16, jnp.float32
    ids = jnp.where(slots[0] >= 0, cluster_ids[0], clusters).astype(wide)
    ids = jnp.broadcast_to(ids[:, None, :], (heads_here, 8, tokens))
    anywhere = pl.BlockSpec(memory_space=pl.ANY)
    dma = pltpu.SemaphoreType.DMA
    token_grad = jax.ShapeDtypeStruct((tokens, cols), low)
    query_grad, key_grad, value_grad, weight, dirs = pl.pallas_call(
        functools.partial(exchange, sources, tokens, width, model, clusters),
        out_shape=(
            token_grad, token_grad, token_grad,
            jax.ShapeDtypeStruct((3, model // sources, cols), wide),
            jax.ShapeDtypeStruct((heads_here, width), wide),
        ),
        in_specs=[anywhere] * 6,
        out_specs=(anywhere,) * 4 + (pl.BlockSpec(memory_space=pltpu.VMEM),),
        scratch_shapes=[
            pltpu.VMEM((4, every, width), low),
            pltpu.VMEM((sources, 8, tokens), wide),
            pltpu.VMEM((every, 2 * width), low),
            pltpu.VMEM((every, 2 * width), low),
            pltpu.VMEM((every, width), wide),
            pltpu.VMEM((every // chunk, every, chunk), wide),
            pltpu.VMEM((every, width), wide),
            pltpu.VMEM((every, width), wide),
            pltpu.VMEM((3, every, width), low),
            pltpu.VMEM((3, tokens, cols), low),
            pltpu.VMEM((tokens, model), low),
            pltpu.VMEM((model, tokens), low),
            pltpu.VMEM((sources, 3, half, cols), low),
            pltpu.VMEM((sources, 3, half, cols), low),
            pltpu.VMEM((sources, 3, half, cols), low),
            pltpu.VMEM((sources, 3, half, cols), low),
            pltpu.VMEM((sources, 3, half, cols), low),
            pltpu.VMEM((2, 3, half, cols), wide),
            pltpu.VMEM((8, width), wide),
            pltpu.VMEM((8, width), wide),
            pltpu.VMEM((sources, 8, width), wide),
            dma((4, sources - 1)), dma((4, sources - 1)),
            dma((sources - 1,)), dma((sources - 1,)), dma((5,)),
            dma((3, sources - 1)), dma((3, sources - 1)),
            dma((sources,)), dma((sources,)),
            dma((sources,)), dma((sources,)), dma((sources,)),
            dma, dma,
            dma((sources,)), dma((sources,)), dma((10,)),
        ],
        compiler_params=pltpu.CompilerParams(
            collective_id=0, has_side_effects=True, vmem_limit_bytes=60 * 1024 * 1024
        ),
    )(layer_input[0], queries[0], keys[0], values[0], out_grad[0], ids)
    return (
        query_grad[None], key_grad[None], value_grad[None],
        weight.transpose(1, 0, 2), dirs[:, None, :],
    )


def for_sending(value):
    return jax.tree.map(lambda a: a.astype(jnp.bfloat16) if a.dtype == jnp.float32 else a, value)


def contract_rows(left, right):
    return lax.dot_general(
        left, right, (((0,), (0,)), ((), ())), preferred_element_type=jnp.float32
    )


def contract_cols(left, right):
    return lax.dot_general(
        left, right, (((1,), (1,)), ((), ())), preferred_element_type=jnp.float32
    )


def unit_rows(array):
    wide = array.astype(jnp.float32)
    return wide * lax.rsqrt(jnp.mean(wide * wide, axis=-1, keepdims=True) + 1e-06)


def block_backward(block, live, rows):
    width = block.shape[1] // 4
    scale = width ** (-0.5)
    query = block[:, :width]
    key = block[:, width : 2 * width]
    value = block[:, 2 * width : 3 * width]
    grad = block[:, 3 * width :]
    key_total = jnp.zeros((block.shape[0], width), jnp.float32)
    value_total = jnp.zeros((block.shape[0], width), jnp.float32)
    query_parts = []
    for start in range(0, block.shape[0], rows):
        query_rows = query[start : start + rows]
        grad_rows = grad[start : start + rows]
        scores = contract_cols(query_rows, key) * scale
        scores = jnp.where(live[None, :], scores, -1e30)
        top = jnp.max(scores, axis=1, keepdims=True)
        weights = jnp.exp(scores - top)
        probs = weights / jnp.sum(weights, axis=1, keepdims=True)
        probs_low = probs.astype(jnp.bfloat16)
        recomputed = jnp.dot(probs_low, value, preferred_element_type=jnp.float32)
        delta = jnp.sum(grad_rows.astype(jnp.float32) * recomputed, axis=1, keepdims=True)
        dprobs = contract_cols(grad_rows, value)
        dscores = (probs * (dprobs - delta)).astype(jnp.bfloat16)
        query_parts.append(jnp.dot(dscores, key, preferred_element_type=jnp.float32) * scale)
        key_total = key_total + contract_rows(dscores, query_rows)
        value_total = value_total + contract_rows(probs_low, grad_rows)
    query_total = jnp.concatenate(query_parts, axis=0)
    return jnp.concatenate((query_total, key_total * scale, value_total), axis=1).astype(
        jnp.bfloat16
    )


def by_cluster(layer_input, queries, keys, values, out_grad, cluster_ids, slots, counts):
    sources = lax.axis_size("seq")
    heads_here = cluster_ids.shape[1]
    tokens_here = queries.shape[1]
    width = queries.shape[2] // heads_here
    clusters_here = counts.shape[2]
    reserved = CAP // sources
    block_rows = clusters_here * reserved
    total_rows = sources * block_rows

    def per_head(array):
        return array[0].reshape(tokens_here, heads_here, width).transpose(1, 0, 2)

    query_heads = per_head(queries)
    key_heads = per_head(keys)
    rows = jnp.concatenate((query_heads, key_heads, per_head(values), per_head(out_grad)), axis=2)
    cluster = cluster_ids[0]
    slot = slots[0]
    kept = slot >= 0
    place = jnp.where(kept, cluster * reserved + slot % reserved, total_rows)

    def fill(row_set, spots):
        return (
            jnp.zeros((total_rows + 1, row_set.shape[1]), row_set.dtype)
            .at[spots]
            .set(row_set)[:total_rows]
        )

    outgoing = jax.vmap(fill)(rows, place).reshape(heads_here, sources, block_rows, 4 * width)
    within = jnp.arange(reserved, dtype=jnp.int32)
    live = (within[None, None, None, :] < counts[0][..., None]).reshape(
        heads_here, clusters_here, CAP
    )
    arrived = lax.all_to_all(outgoing, "seq", split_axis=1, concat_axis=1, tiled=True)
    number = arrived.shape[0]
    blocks = arrived.reshape(number, sources, clusters_here, reserved, 4 * width)
    blocks = blocks.transpose(0, 2, 1, 3, 4).reshape(number * clusters_here, CAP, 4 * width)
    flat_mask = live.reshape(number * clusters_here, CAP)
    grads = lax.map(
        lambda item: block_backward(item[0], item[1], min(CAP, 512)), (blocks, flat_mask)
    )
    home = grads.reshape(number, clusters_here, sources, reserved, 3 * width)
    home = home.transpose(0, 2, 1, 3, 4).reshape(number, sources, block_rows, 3 * width)
    unit = (unit_rows(blocks[..., :width]) + unit_rows(blocks[..., width : 2 * width])) * flat_mask[
        ..., None
    ].astype(jnp.float32)
    sums = jnp.sum(unit, axis=1).reshape(number, clusters_here, width)
    home, owner_total = (home, sums)
    returned = lax.all_to_all(
        for_sending(home), "seq", split_axis=1, concat_axis=1, tiled=True
    ).astype(home.dtype)
    padded = jnp.concatenate(
        (
            returned.reshape(heads_here, total_rows, 3 * width),
            jnp.zeros((heads_here, 1, 3 * width), returned.dtype),
        ),
        axis=1,
    )
    back = jax.vmap(lambda table, spots: table[spots])(padded, place)

    def token_major(part):
        return part.transpose(1, 0, 2).reshape(tokens_here, heads_here * width)

    query_grad = token_major(back[:, :, :width])
    key_grad = token_major(back[:, :, width : 2 * width])
    value_grad = token_major(back[:, :, 2 * width :])
    stacked = jnp.stack((query_grad, key_grad, value_grad), axis=1).reshape(
        tokens_here, 3 * heads_here * width
    )
    inputs = layer_input[0]
    weight_share = lax.psum_scatter(
        contract_rows(inputs, stacked)
        .reshape(lax.axis_size("seq") * (inputs.shape[1] // sources), 3, heads_here * width)
        .astype(jnp.bfloat16),
        "seq",
        scatter_dimension=0,
        tiled=True,
    )
    unit = (unit_rows(query_heads) + unit_rows(key_heads)) * kept[..., None].astype(jnp.float32)
    member = (cluster[..., None] == jnp.arange(sources * clusters_here, dtype=jnp.int32)).astype(
        jnp.float32
    )
    term = jnp.einsum("htc,hte->hce", member, unit, precision=lax.Precision.HIGHEST)
    centroid_part = lax.psum_scatter(
        term.astype(jnp.bfloat16), "seq", scatter_dimension=1, tiled=True
    )
    weight_grad, centroid_total = (
        lax.psum(weight_share, "dp").astype(jnp.float32),
        lax.psum(centroid_part, "dp").astype(jnp.float32),
    )
    centroid_dirs = centroid_total * lax.rsqrt(
        jnp.mean(centroid_total * centroid_total, axis=-1, keepdims=True) + 1e-06
    )
    return (query_grad[None], key_grad[None], value_grad[None], weight_grad, centroid_dirs)


def on_device(*arrays):
    cluster_ids, counts = arrays[5], arrays[7]
    sources = lax.axis_size("seq")
    if cluster_ids.shape[1] == sources and counts.shape[2] == 1 and sources <= 8:
        return by_head(*arrays)
    return by_cluster(*arrays)


def solution(mesh):
    return jax.shard_map(
        on_device,
        mesh=mesh,
        in_specs=(
            P(("groups", "dp"), "seq", None),
            P(("groups", "dp"), "seq", "clus"),
            P(("groups", "dp"), "seq", "clus"),
            P(("groups", "dp"), "seq", "clus"),
            P(("groups", "dp"), "seq", "clus"),
            P(("groups", "dp"), "clus", "seq"),
            P(("groups", "dp"), "clus", "seq"),
            P(("groups", "dp"), "clus", "seq", None),
        ),
        out_specs=(
            P(("groups", "dp"), "seq", "clus"),
            P(("groups", "dp"), "seq", "clus"),
            P(("groups", "dp"), "seq", "clus"),
            P(("groups", "seq"), None, "clus"),
            P(("groups", "clus"), "seq", None),
        ),
        check_vma=False,
    )
```

```python
import functools

import jax
import jax.numpy as jnp
from jax import lax
from jax.experimental import pallas as pl
from jax.experimental.pallas import tpu as pltpu
from jax.sharding import PartitionSpec as P

CAP = 1024
MESH = pl.DeviceIdType.MESH
LOG2E = 1.4426950408889634
FAR = 131072.0


def dot(left, right, left_dim, right_dim):
    return lax.dot_general(
        left, right, (((left_dim,), (right_dim,)), ((), ())), preferred_element_type=jnp.float32
    )


def exchange(
    sources, tokens, width, model, clusters,
    layer, queries, keys, values, grads, ids,
    query_out, key_out, value_out, weight_out, dirs_out,
    rows, ids_all, query_wide, key_wide, keep, probs, key_sum, back, landed,
    layer_rows, layer_cols, sib_term, sib_in, term, from_left, from_right, total,
    cent_mine, cent_sib, cent_all,
    row_send, row_recv, id_send, id_recv, local_sem, back_send, back_recv,
    sib_send, sib_recv, hop_send, left_recv, right_recv, half_send, half_recv,
    cent_send, cent_recv, out_sem, store_sem,
):
    me = lax.axis_index("seq")
    core = lax.axis_index("dp")
    other = 1 - core
    scale = width ** (-0.5)
    peers = [lax.rem(me + step, sources) for step in range(1, sources)]
    my_rows = pl.ds(pl.multiple_of(me * tokens, tokens), tokens)
    my_cols = pl.ds(pl.multiple_of(me * width, width), width)
    stream = (queries, keys, values, grads)
    half = model // sources // 2
    every = sources * tokens

    layer_in = pltpu.make_async_copy(layer, layer_rows, out_sem.at[0])
    layer_in.start()
    barrier = pltpu.get_barrier_semaphore()
    for peer in peers:
        pl.semaphore_signal(barrier, inc=1, device_id={"seq": peer}, device_id_type=MESH)
    pl.semaphore_signal(barrier, inc=1, device_id={"dp": other}, device_id_type=MESH)
    pl.semaphore_wait(barrier, sources)

    def remote(src, dst, send, recv, target):
        copy = pltpu.make_async_remote_copy(
            src_ref=src, dst_ref=dst, send_sem=send, recv_sem=recv,
            device_id=target, device_id_type=MESH,
        )
        copy.start()
        return copy

    id_copies = [
        remote(ids.at[peer], ids_all.at[me], id_send.at[n], id_recv.at[n], {"seq": peer})
        for n, peer in enumerate(peers)
    ]
    row_copies = [None] * 4
    for t in (0, 1, 3, 2):
        copies = []
        for n, peer in enumerate(peers):
            cols = pl.ds(pl.multiple_of(peer * width, width), width)
            copies.append(
                remote(
                    stream[t].at[:, cols], rows.at[t, my_rows, :],
                    row_send.at[t, n], row_recv.at[t, n], {"seq": peer},
                )
            )
        row_copies[t] = copies
    local = [
        pltpu.make_async_copy(stream[t].at[:, my_cols], rows.at[t, my_rows, :], local_sem.at[t])
        for t in range(4)
    ]
    local.append(pltpu.make_async_copy(ids.at[me], ids_all.at[me], local_sem.at[4]))
    for copy in local:
        copy.start()

    layer_in.wait()
    piece = 256

    def turn(n, carry):
        cols = pl.ds(pl.multiple_of(n * piece, piece), piece)
        layer_cols[cols, :] = layer_rows[:, cols].T
        return carry

    lax.fori_loop(0, model // piece, turn, 0)

    local[4].wait()
    for copy in id_copies:
        copy.wait()
    lane = lax.broadcasted_iota(jnp.int32, (128, 128), 1)
    sub = lax.broadcasted_iota(jnp.int32, (128, 128), 0)
    eye = jnp.where(lane == sub, 1.0, 0.0).astype(jnp.bfloat16)
    inside = jnp.where(sub < clusters, 1.0, 0.0).astype(jnp.bfloat16)
    level = lax.broadcasted_iota(jnp.int32, (128, tokens), 0).astype(jnp.float32)

    for t in range(2):
        local[t].wait()
        for copy in row_copies[t]:
            copy.wait()

    def unit(array):
        wide = array.astype(jnp.float32)
        return wide * lax.rsqrt(jnp.mean(wide * wide, axis=-1, keepdims=True) + 1e-06)

    cent = jnp.zeros((128, width), jnp.float32)
    for s in range(sources):
        span = slice(s * tokens, (s + 1) * tokens)
        member = jnp.where(level == ids_all[s, 0:1, :], 1.0, 0.0).astype(jnp.bfloat16)
        column = dot(member, eye, 0, 0)
        keep[span, :] = dot(member, inside, 0, 0)
        query_wide[span, :width] = rows[0, span, :]
        key_wide[span, :width] = rows[1, span, :]
        query_wide[span, width:] = column.astype(jnp.bfloat16)
        key_wide[span, width:] = ((column - 1.0) * FAR).astype(jnp.bfloat16)
        both = unit(rows[0, span, :]) + unit(rows[1, span, :])
        high = both.astype(jnp.bfloat16)
        low = (both - high.astype(jnp.float32)).astype(jnp.bfloat16)
        cent = cent + dot(member, high, 1, 0) + dot(member, low, 1, 0)
    cent_mine[...] = cent[: cent_mine.shape[0], :]
    cent_first = remote(cent_mine, cent_sib, cent_send.at[0], cent_recv.at[0], {"dp": other})

    chunk = probs.shape[2]
    chunks = every // chunk

    def soft(n, carry):
        span = pl.ds(pl.multiple_of(n * chunk, chunk), chunk)
        scores = dot(key_wide[...], query_wide[span, :], 1, 1)
        top = jnp.max(scores, axis=0, keepdims=True)
        weights = jnp.exp2((scores - top) * (scale * LOG2E))
        probs[n] = weights * (1.0 / jnp.sum(weights, axis=0, keepdims=True))
        return carry

    lax.fori_loop(0, chunks, soft, 0)

    cent_first.wait()
    cent_all[me] = cent_mine[...] + cent_sib[...]
    cent_copies = [
        remote(
            cent_all.at[me], cent_all.at[me], cent_send.at[n + 1], cent_recv.at[n + 1],
            {"seq": peer},
        )
        for n, peer in enumerate(peers)
    ]
    def give_back(t, step, peer):
        span = pl.ds(pl.multiple_of(peer * tokens, tokens), tokens)
        return pltpu.make_async_remote_copy(
            src_ref=back.at[t, span, :], dst_ref=landed.at[t, :, my_cols],
            send_sem=back_send.at[t, step], recv_sem=back_recv.at[t, step],
            device_id={"seq": peer}, device_id_type=MESH,
        )

    def arrive(t):
        local[t].wait()
        for copy in row_copies[t]:
            copy.wait()

    arrive(3)
    for step in range(sources):
        source = peers[step] if step < sources - 1 else me
        span = pl.ds(pl.multiple_of(source * tokens, tokens), tokens)
        gathered = jnp.zeros((tokens, width), jnp.float32)
        for n in range(chunks):
            gathered = gathered + dot(
                probs[n, span, :].astype(jnp.bfloat16), rows[3, n * chunk : (n + 1) * chunk, :], 1, 0
            )
        back[2, span, :] = (gathered * keep[span, :]).astype(jnp.bfloat16)
        if step < sources - 1:
            give_back(2, step, source).start()
        else:
            landed[2, :, my_cols] = back[2, span, :]

    arrive(2)
    key_sum[...] = jnp.zeros_like(key_sum)
    each = tokens // chunk

    def backward(index, carry):
        step = index // each
        source = lax.rem(me + 1 + step, sources)
        n = source * each + lax.rem(index, each)
        span = pl.ds(pl.multiple_of(n * chunk, chunk), chunk)
        share = probs[n]
        share_low = share.astype(jnp.bfloat16)
        dprobs = dot(rows[2], rows[3, span, :], 1, 1)
        delta = jnp.sum(share_low.astype(jnp.float32) * dprobs, axis=0, keepdims=True)
        dscores = (share * (dprobs - delta)).astype(jnp.bfloat16)
        query_part = dot(dscores, rows[1], 0, 0)
        back[0, span, :] = (query_part * (keep[span, :] * scale)).astype(jnp.bfloat16)
        key_sum[...] += dot(dscores, rows[0, span, :], 1, 0)

        @pl.when(jnp.logical_and(lax.rem(index, each) == each - 1, step < sources - 1))
        def _():
            give_back(0, step, source).start()

        return carry

    lax.fori_loop(0, chunks, backward, 0)
    landed[0, :, my_cols] = back[0, my_rows, :]
    back[1] = (key_sum[...] * (keep[...] * scale)).astype(jnp.bfloat16)
    for step, peer in enumerate(peers):
        give_back(1, step, peer).start()
    landed[1, :, my_cols] = back[1, my_rows, :]

    outs = []

    def collect(t):
        for step, peer in enumerate(peers):
            give_back(t, step, peer).wait()
        copy = pltpu.make_async_copy(
            landed.at[t], (query_out, key_out, value_out)[t], out_sem.at[t + 1]
        )
        copy.start()
        outs.append(copy)

    near_start = me < sources // 2
    order = []
    for k in range(sources // 2):
        order.append(jnp.where(near_start, sources - 1 - k, k))
        order.append(jnp.where(near_start, k, sources - 1 - k))

    def part(d, side, t):
        span = pl.ds(pl.multiple_of(d * (2 * half) + side * half, half), half)
        return dot(layer_cols[span, :], landed[t], 1, 0).astype(jnp.bfloat16)

    def across(t, d):
        return pltpu.make_async_remote_copy(
            src_ref=sib_term.at[d, t], dst_ref=sib_in.at[d, t],
            send_sem=sib_send.at[d, t], recv_sem=sib_recv.at[d, t],
            device_id={"dp": other}, device_id_type=MESH,
        )

    def terms(t):
        collect(t)
        for d in order:
            sib_term[d, t] = part(d, other, t)
            across(t, d).start()
        for d in order:
            term[d, t] = part(d, core, t)

    def hop(t, d, side):
        landing, arrival = (from_left, left_recv) if side > 0 else (from_right, right_recv)
        return pltpu.make_async_remote_copy(
            src_ref=term.at[d, t], dst_ref=landing.at[d, t],
            send_sem=hop_send.at[d, t], recv_sem=arrival.at[d, t],
            device_id={"seq": me + side}, device_id_type=MESH,
        )

    last = sources - 1

    def add(t, d, arrived):
        term[d, t] = (
            term[d, t].astype(jnp.float32) + arrived[d, t].astype(jnp.float32)
        ).astype(jnp.bfloat16)

    def hops(t):
        for d in order:
            across(t, d).wait_recv()
            add(t, d, sib_in)

            @pl.when(jnp.logical_and(me < d, me > 0))
            def _():
                hop(t, d, 1).wait_recv()
                add(t, d, from_left)

            @pl.when(jnp.logical_and(me > d, me < last))
            def _():
                hop(t, d, -1).wait_recv()
                add(t, d, from_right)

            @pl.when(me < d)
            def _():
                hop(t, d, 1).start()

            @pl.when(me > d)
            def _():
                hop(t, d, -1).start()

    def store(side, t):
        copy = pltpu.make_async_copy(
            total.at[side, t],
            weight_out.at[t, pl.ds(pl.multiple_of(side * half, half), half), :],
            store_sem.at[side, t],
        )
        copy.start()
        outs.append(copy)

    finals = {}

    def finish(t):
        total[core, t] = term[me, t].astype(jnp.float32)

        @pl.when(me > 0)
        def _():
            hop(t, me, 1).wait_recv()
            total[core, t] += from_left[me, t].astype(jnp.float32)

        @pl.when(me < last)
        def _():
            hop(t, me, -1).wait_recv()
            total[core, t] += from_right[me, t].astype(jnp.float32)

        finals[t] = remote(
            total.at[core, t], total.at[core, t], half_send.at[t], half_recv.at[t], {"dp": other}
        )
        store(core, t)

    terms(2)
    terms(0)
    hops(2)
    terms(1)
    hops(0)
    finish(2)
    hops(1)
    finish(0)
    for copy in cent_copies:
        copy.wait()
    sums = [cent_all[h, pl.ds(me, 1), :] for h in range(sources)]
    sums = jnp.concatenate(sums, axis=0)
    dirs_out[...] = sums * lax.rsqrt(jnp.mean(sums * sums, axis=-1, keepdims=True) + 1e-06)
    finish(1)
    for t in (2, 0, 1):
        for d in order:
            across(t, d).wait_send()

            @pl.when(me < d)
            def _():
                hop(t, d, 1).wait_send()

            @pl.when(me > d)
            def _():
                hop(t, d, -1).wait_send()

    for t in (2, 0, 1):
        finals[t].wait()
        store(other, t)
    for copy in outs:
        copy.wait()


def settle(*refs):
    count = len(refs) // 2
    copies = [
        pltpu.make_async_copy(refs[i], refs[count + i], refs[-1].at[i]) for i in range(count)
    ]
    for copy in copies:
        copy.start()
    for copy in copies:
        copy.wait()


def by_head(layer_input, queries, keys, values, out_grad, cluster_ids, slots, counts):
    sources = lax.axis_size("seq")
    heads_here = cluster_ids.shape[1]
    tokens = queries.shape[1]
    width = queries.shape[2] // heads_here
    model = layer_input.shape[2]
    clusters = sources * counts.shape[2]
    every = sources * tokens
    half = model // sources // 2
    cols = heads_here * width
    chunk = 256
    low, wide = jnp.bfloat16, jnp.float32
    ids = jnp.where(slots[0] >= 0, cluster_ids[0], clusters).astype(wide)
    ids = jnp.broadcast_to(ids[:, None, :], (heads_here, 8, tokens))
    anywhere = pl.BlockSpec(memory_space=pl.ANY)
    dma = pltpu.SemaphoreType.DMA
    token_grad = jax.ShapeDtypeStruct((tokens, cols), low)
    results = pl.pallas_call(
        functools.partial(exchange, sources, tokens, width, model, clusters),
        out_shape=(
            token_grad, token_grad, token_grad,
            jax.ShapeDtypeStruct((3, model // sources, cols), wide),
            jax.ShapeDtypeStruct((heads_here, width), wide),
        ),
        in_specs=[anywhere] * 6,
        out_specs=(anywhere,) * 4 + (pl.BlockSpec(memory_space=pltpu.VMEM),),
        scratch_shapes=[
            pltpu.VMEM((4, every, width), low),
            pltpu.VMEM((sources, 8, tokens), wide),
            pltpu.VMEM((every, 2 * width), low),
            pltpu.VMEM((every, 2 * width), low),
            pltpu.VMEM((every, width), wide),
            pltpu.VMEM((every // chunk, every, chunk), wide),
            pltpu.VMEM((every, width), wide),
            pltpu.VMEM((3, every, width), low),
            pltpu.VMEM((3, tokens, cols), low),
            pltpu.VMEM((tokens, model), low),
            pltpu.VMEM((model, tokens), low),
            pltpu.VMEM((sources, 3, half, cols), low),
            pltpu.VMEM((sources, 3, half, cols), low),
            pltpu.VMEM((sources, 3, half, cols), low),
            pltpu.VMEM((sources, 3, half, cols), low),
            pltpu.VMEM((sources, 3, half, cols), low),
            pltpu.VMEM((2, 3, half, cols), wide),
            pltpu.VMEM((8, width), wide),
            pltpu.VMEM((8, width), wide),
            pltpu.VMEM((sources, 8, width), wide),
            dma((4, sources - 1)), dma((4, sources - 1)),
            dma((sources - 1,)), dma((sources - 1,)), dma((5,)),
            dma((3, sources - 1)), dma((3, sources - 1)),
            dma((sources, 3)), dma((sources, 3)),
            dma((sources, 3)), dma((sources, 3)), dma((sources, 3)),
            dma((3,)), dma((3,)),
            dma((sources,)), dma((sources,)), dma((4,)), dma((2, 3)),
        ],
        compiler_params=pltpu.CompilerParams(
            collective_id=0, has_side_effects=True, vmem_limit_bytes=60 * 1024 * 1024
        ),
    )(layer_input[0], queries[0], keys[0], values[0], out_grad[0], ids)
    query_grad, key_grad, value_grad, weight, dirs = pl.pallas_call(
        settle,
        out_shape=tuple(jax.ShapeDtypeStruct(a.shape, a.dtype) for a in results),
        in_specs=[anywhere] * 5,
        out_specs=(anywhere,) * 5,
        scratch_shapes=[dma((5,))],
    )(*results)
    return (
        query_grad[None], key_grad[None], value_grad[None],
        weight.transpose(1, 0, 2), dirs[:, None, :],
    )


def for_sending(value):
    return jax.tree.map(lambda a: a.astype(jnp.bfloat16) if a.dtype == jnp.float32 else a, value)


def contract_rows(left, right):
    return lax.dot_general(
        left, right, (((0,), (0,)), ((), ())), preferred_element_type=jnp.float32
    )


def contract_cols(left, right):
    return lax.dot_general(
        left, right, (((1,), (1,)), ((), ())), preferred_element_type=jnp.float32
    )


def unit_rows(array):
    wide = array.astype(jnp.float32)
    return wide * lax.rsqrt(jnp.mean(wide * wide, axis=-1, keepdims=True) + 1e-06)


def block_backward(block, live, rows):
    width = block.shape[1] // 4
    scale = width ** (-0.5)
    query = block[:, :width]
    key = block[:, width : 2 * width]
    value = block[:, 2 * width : 3 * width]
    grad = block[:, 3 * width :]
    key_total = jnp.zeros((block.shape[0], width), jnp.float32)
    value_total = jnp.zeros((block.shape[0], width), jnp.float32)
    query_parts = []
    for start in range(0, block.shape[0], rows):
        query_rows = query[start : start + rows]
        grad_rows = grad[start : start + rows]
        scores = contract_cols(query_rows, key) * scale
        scores = jnp.where(live[None, :], scores, -1e30)
        top = jnp.max(scores, axis=1, keepdims=True)
        weights = jnp.exp(scores - top)
        probs = weights / jnp.sum(weights, axis=1, keepdims=True)
        probs_low = probs.astype(jnp.bfloat16)
        recomputed = jnp.dot(probs_low, value, preferred_element_type=jnp.float32)
        delta = jnp.sum(grad_rows.astype(jnp.float32) * recomputed, axis=1, keepdims=True)
        dprobs = contract_cols(grad_rows, value)
        dscores = (probs * (dprobs - delta)).astype(jnp.bfloat16)
        query_parts.append(jnp.dot(dscores, key, preferred_element_type=jnp.float32) * scale)
        key_total = key_total + contract_rows(dscores, query_rows)
        value_total = value_total + contract_rows(probs_low, grad_rows)
    query_total = jnp.concatenate(query_parts, axis=0)
    return jnp.concatenate((query_total, key_total * scale, value_total), axis=1).astype(
        jnp.bfloat16
    )


def by_cluster(layer_input, queries, keys, values, out_grad, cluster_ids, slots, counts):
    sources = lax.axis_size("seq")
    heads_here = cluster_ids.shape[1]
    tokens_here = queries.shape[1]
    width = queries.shape[2] // heads_here
    clusters_here = counts.shape[2]
    reserved = CAP // sources
    block_rows = clusters_here * reserved
    total_rows = sources * block_rows

    def per_head(array):
        return array[0].reshape(tokens_here, heads_here, width).transpose(1, 0, 2)

    query_heads = per_head(queries)
    key_heads = per_head(keys)
    rows = jnp.concatenate((query_heads, key_heads, per_head(values), per_head(out_grad)), axis=2)
    cluster = cluster_ids[0]
    slot = slots[0]
    kept = slot >= 0
    place = jnp.where(kept, cluster * reserved + slot % reserved, total_rows)

    def fill(row_set, spots):
        return (
            jnp.zeros((total_rows + 1, row_set.shape[1]), row_set.dtype)
            .at[spots]
            .set(row_set)[:total_rows]
        )

    outgoing = jax.vmap(fill)(rows, place).reshape(heads_here, sources, block_rows, 4 * width)
    within = jnp.arange(reserved, dtype=jnp.int32)
    live = (within[None, None, None, :] < counts[0][..., None]).reshape(
        heads_here, clusters_here, CAP
    )
    arrived = lax.all_to_all(outgoing, "seq", split_axis=1, concat_axis=1, tiled=True)
    number = arrived.shape[0]
    blocks = arrived.reshape(number, sources, clusters_here, reserved, 4 * width)
    blocks = blocks.transpose(0, 2, 1, 3, 4).reshape(number * clusters_here, CAP, 4 * width)
    flat_mask = live.reshape(number * clusters_here, CAP)
    grads = lax.map(
        lambda item: block_backward(item[0], item[1], min(CAP, 512)), (blocks, flat_mask)
    )
    home = grads.reshape(number, clusters_here, sources, reserved, 3 * width)
    home = home.transpose(0, 2, 1, 3, 4).reshape(number, sources, block_rows, 3 * width)
    unit = (unit_rows(blocks[..., :width]) + unit_rows(blocks[..., width : 2 * width])) * flat_mask[
        ..., None
    ].astype(jnp.float32)
    sums = jnp.sum(unit, axis=1).reshape(number, clusters_here, width)
    home, owner_total = (home, sums)
    returned = lax.all_to_all(
        for_sending(home), "seq", split_axis=1, concat_axis=1, tiled=True
    ).astype(home.dtype)
    padded = jnp.concatenate(
        (
            returned.reshape(heads_here, total_rows, 3 * width),
            jnp.zeros((heads_here, 1, 3 * width), returned.dtype),
        ),
        axis=1,
    )
    back = jax.vmap(lambda table, spots: table[spots])(padded, place)

    def token_major(part):
        return part.transpose(1, 0, 2).reshape(tokens_here, heads_here * width)

    query_grad = token_major(back[:, :, :width])
    key_grad = token_major(back[:, :, width : 2 * width])
    value_grad = token_major(back[:, :, 2 * width :])
    stacked = jnp.stack((query_grad, key_grad, value_grad), axis=1).reshape(
        tokens_here, 3 * heads_here * width
    )
    inputs = layer_input[0]
    weight_share = lax.psum_scatter(
        contract_rows(inputs, stacked)
        .reshape(lax.axis_size("seq") * (inputs.shape[1] // sources), 3, heads_here * width)
        .astype(jnp.bfloat16),
        "seq",
        scatter_dimension=0,
        tiled=True,
    )
    unit = (unit_rows(query_heads) + unit_rows(key_heads)) * kept[..., None].astype(jnp.float32)
    member = (cluster[..., None] == jnp.arange(sources * clusters_here, dtype=jnp.int32)).astype(
        jnp.float32
    )
    term = jnp.einsum("htc,hte->hce", member, unit, precision=lax.Precision.HIGHEST)
    centroid_part = lax.psum_scatter(
        term.astype(jnp.bfloat16), "seq", scatter_dimension=1, tiled=True
    )
    weight_grad, centroid_total = (
        lax.psum(weight_share, "dp").astype(jnp.float32),
        lax.psum(centroid_part, "dp").astype(jnp.float32),
    )
    centroid_dirs = centroid_total * lax.rsqrt(
        jnp.mean(centroid_total * centroid_total, axis=-1, keepdims=True) + 1e-06
    )
    return (query_grad[None], key_grad[None], value_grad[None], weight_grad, centroid_dirs)


def on_device(*arrays):
    cluster_ids, counts = arrays[5], arrays[7]
    sources = lax.axis_size("seq")
    if cluster_ids.shape[1] == sources and counts.shape[2] == 1 and sources <= 8:
        return by_head(*arrays)
    return by_cluster(*arrays)


def solution(mesh):
    return jax.shard_map(
        on_device,
        mesh=mesh,
        in_specs=(
            P(("groups", "dp"), "seq", None),
            P(("groups", "dp"), "seq", "clus"),
            P(("groups", "dp"), "seq", "clus"),
            P(("groups", "dp"), "seq", "clus"),
            P(("groups", "dp"), "seq", "clus"),
            P(("groups", "dp"), "clus", "seq"),
            P(("groups", "dp"), "clus", "seq"),
            P(("groups", "dp"), "clus", "seq", None),
        ),
        out_specs=(
            P(("groups", "dp"), "seq", "clus"),
            P(("groups", "dp"), "seq", "clus"),
            P(("groups", "dp"), "seq", "clus"),
            P(("groups", "seq"), None, "clus"),
            P(("groups", "clus"), "seq", None),
        ),
        check_vma=False,
    )
```

```python
import functools

import jax
import jax.numpy as jnp
from jax import lax
from jax.experimental import pallas as pl
from jax.experimental.pallas import tpu as pltpu
from jax.sharding import PartitionSpec as P

CAP = 1024
MESH = pl.DeviceIdType.MESH
LOG2E = 1.4426950408889634
FAR = 131072.0


def dot(left, right, left_dim, right_dim):
    return lax.dot_general(
        left, right, (((left_dim,), (right_dim,)), ((), ())), preferred_element_type=jnp.float32
    )


def exchange(
    sources, tokens, width, model, clusters,
    layer, queries, keys, values, grads, cluster, slot,
    query_out, key_out, value_out, weight_out, dirs_out,
    rows, ids, ids_all, query_wide, key_wide, keep, probs, key_sum, back, landed,
    layer_rows, layer_cols, sib_term, sib_in, term, from_left, from_right, total,
    cent_mine, cent_sib, cent_all,
    row_send, row_recv, id_send, id_recv, local_sem, back_send, back_recv,
    sib_send, sib_recv, hop_send, left_recv, right_recv, half_send, half_recv,
    cent_send, cent_recv, out_sem, store_sem,
):
    me = lax.axis_index("seq")
    core = lax.axis_index("dp")
    other = 1 - core
    scale = width ** (-0.5)
    peers = [lax.rem(me + step, sources) for step in range(1, sources)]
    my_rows = pl.ds(pl.multiple_of(me * tokens, tokens), tokens)
    my_cols = pl.ds(pl.multiple_of(me * width, width), width)
    stream = (queries, keys, values, grads)
    half = model // sources // 2
    every = sources * tokens

    named = jnp.where(slot[...] >= 0, cluster[...], clusters).astype(jnp.float32)
    for h in range(sources):
        ids[h] = jnp.broadcast_to(named[h : h + 1, :], (8, tokens))
    layer_in = pltpu.make_async_copy(layer, layer_rows, out_sem.at[0])
    layer_in.start()
    barrier = pltpu.get_barrier_semaphore()
    for peer in peers:
        pl.semaphore_signal(barrier, inc=1, device_id={"seq": peer}, device_id_type=MESH)
    pl.semaphore_signal(barrier, inc=1, device_id={"dp": other}, device_id_type=MESH)
    pl.semaphore_wait(barrier, sources)

    def remote(src, dst, send, recv, target):
        copy = pltpu.make_async_remote_copy(
            src_ref=src, dst_ref=dst, send_sem=send, recv_sem=recv,
            device_id=target, device_id_type=MESH,
        )
        copy.start()
        return copy

    id_copies = [
        remote(ids.at[peer], ids_all.at[me], id_send.at[n], id_recv.at[n], {"seq": peer})
        for n, peer in enumerate(peers)
    ]
    row_copies = [None] * 4

    def leave(t):
        copies = []
        for n, peer in enumerate(peers):
            cols = pl.ds(pl.multiple_of(peer * width, width), width)
            copies.append(
                remote(
                    stream[t].at[:, cols], rows.at[t, my_rows, :],
                    row_send.at[t, n], row_recv.at[t, n], {"seq": peer},
                )
            )
        row_copies[t] = copies

    leave(0)
    leave(1)
    local = [
        pltpu.make_async_copy(stream[t].at[:, my_cols], rows.at[t, my_rows, :], local_sem.at[t])
        for t in range(4)
    ]
    local.append(pltpu.make_async_copy(ids.at[me], ids_all.at[me], local_sem.at[4]))
    for copy in local:
        copy.start()

    layer_in.wait()
    piece = 256

    def turn(n, carry):
        cols = pl.ds(pl.multiple_of(n * piece, piece), piece)
        layer_cols[cols, :] = layer_rows[:, cols].T
        return carry

    lax.fori_loop(0, model // piece, turn, 0)

    local[4].wait()
    for copy in id_copies:
        copy.wait()
    lane = lax.broadcasted_iota(jnp.int32, (128, 128), 1)
    sub = lax.broadcasted_iota(jnp.int32, (128, 128), 0)
    eye = jnp.where(lane == sub, 1.0, 0.0).astype(jnp.bfloat16)
    inside = jnp.where(sub < clusters, 1.0, 0.0).astype(jnp.bfloat16)
    level = lax.broadcasted_iota(jnp.int32, (128, tokens), 0).astype(jnp.float32)

    for t in range(2):
        for copy in row_copies[t]:
            copy.wait_send()
    leave(3)
    leave(2)
    for t in range(2):
        local[t].wait()
        for copy in row_copies[t]:
            copy.wait_recv()

    def unit(array):
        wide = array.astype(jnp.float32)
        return wide * lax.rsqrt(jnp.mean(wide * wide, axis=-1, keepdims=True) + 1e-06)

    cent = jnp.zeros((128, width), jnp.float32)
    for s in range(sources):
        span = slice(s * tokens, (s + 1) * tokens)
        member = jnp.where(level == ids_all[s, 0:1, :], 1.0, 0.0).astype(jnp.bfloat16)
        column = dot(member, eye, 0, 0)
        keep[span, :] = dot(member, inside, 0, 0)
        query_wide[span, :width] = rows[0, span, :]
        key_wide[span, :width] = rows[1, span, :]
        query_wide[span, width:] = column.astype(jnp.bfloat16)
        key_wide[span, width:] = ((column - 1.0) * FAR).astype(jnp.bfloat16)
        both = unit(rows[0, span, :]) + unit(rows[1, span, :])
        high = both.astype(jnp.bfloat16)
        low = (both - high.astype(jnp.float32)).astype(jnp.bfloat16)
        cent = cent + dot(member, high, 1, 0) + dot(member, low, 1, 0)
    cent_mine[...] = cent[: cent_mine.shape[0], :]
    cent_first = remote(cent_mine, cent_sib, cent_send.at[0], cent_recv.at[0], {"dp": other})

    chunk = probs.shape[2]
    chunks = every // chunk

    def soft(n, carry):
        span = pl.ds(pl.multiple_of(n * chunk, chunk), chunk)
        scores = dot(key_wide[...], query_wide[span, :], 1, 1)
        top = jnp.max(scores, axis=0, keepdims=True)
        weights = jnp.exp2((scores - top) * (scale * LOG2E))
        probs[n] = weights * (1.0 / jnp.sum(weights, axis=0, keepdims=True))
        return carry

    lax.fori_loop(0, chunks // 2, soft, 0)
    for copy in row_copies[3]:
        copy.wait_send()
    lax.fori_loop(chunks // 2, chunks, soft, 0)
    local[3].wait()
    for copy in row_copies[3]:
        copy.wait_recv()

    cent_first.wait()
    cent_all[me] = cent_mine[...] + cent_sib[...]
    cent_copies = [
        remote(
            cent_all.at[me], cent_all.at[me], cent_send.at[n + 1], cent_recv.at[n + 1],
            {"seq": peer},
        )
        for n, peer in enumerate(peers)
    ]
    def give_back(t, step, peer):
        span = pl.ds(pl.multiple_of(peer * tokens, tokens), tokens)
        return pltpu.make_async_remote_copy(
            src_ref=back.at[t, span, :], dst_ref=landed.at[t, :, my_cols],
            send_sem=back_send.at[t, step], recv_sem=back_recv.at[t, step],
            device_id={"seq": peer}, device_id_type=MESH,
        )

    for step in range(sources):
        source = peers[step] if step < sources - 1 else me
        span = pl.ds(pl.multiple_of(source * tokens, tokens), tokens)
        gathered = jnp.zeros((tokens, width), jnp.float32)
        for n in range(chunks):
            gathered = gathered + dot(
                probs[n, span, :].astype(jnp.bfloat16), rows[3, n * chunk : (n + 1) * chunk, :], 1, 0
            )
        back[2, span, :] = (gathered * keep[span, :]).astype(jnp.bfloat16)
        if step < sources - 1:
            give_back(2, step, source).start()
        else:
            landed[2, :, my_cols] = back[2, span, :]

    local[2].wait()
    for copy in row_copies[2]:
        copy.wait()
    key_sum[...] = jnp.zeros_like(key_sum)
    each = tokens // chunk

    def backward(index, carry):
        step = index // each
        source = lax.rem(me + 1 + step, sources)
        n = source * each + lax.rem(index, each)
        span = pl.ds(pl.multiple_of(n * chunk, chunk), chunk)
        share = probs[n]
        share_low = share.astype(jnp.bfloat16)
        dprobs = dot(rows[2], rows[3, span, :], 1, 1)
        delta = jnp.sum(share_low.astype(jnp.float32) * dprobs, axis=0, keepdims=True)
        dscores = (share * (dprobs - delta)).astype(jnp.bfloat16)
        query_part = dot(dscores, rows[1], 0, 0)
        back[0, span, :] = (query_part * (keep[span, :] * scale)).astype(jnp.bfloat16)
        key_sum[...] += dot(dscores, rows[0, span, :], 1, 0)

        @pl.when(jnp.logical_and(lax.rem(index, each) == each - 1, step < sources - 1))
        def _():
            give_back(0, step, source).start()

        return carry

    lax.fori_loop(0, chunks, backward, 0)
    landed[0, :, my_cols] = back[0, my_rows, :]
    back[1] = (key_sum[...] * (keep[...] * scale)).astype(jnp.bfloat16)
    for step, peer in enumerate(peers):
        give_back(1, step, peer).start()
    landed[1, :, my_cols] = back[1, my_rows, :]

    outs = []

    def collect(t):
        for step, peer in enumerate(peers):
            give_back(t, step, peer).wait()
        copy = pltpu.make_async_copy(
            landed.at[t], (query_out, key_out, value_out)[t], out_sem.at[t + 1]
        )
        copy.start()
        outs.append(copy)

    near_start = me < sources // 2
    order = []
    for k in range(sources // 2):
        order.append(jnp.where(near_start, sources - 1 - k, k))
        order.append(jnp.where(near_start, k, sources - 1 - k))

    def part(d, side, t):
        span = pl.ds(pl.multiple_of(d * (2 * half) + side * half, half), half)
        return dot(layer_cols[span, :], landed[t], 1, 0).astype(jnp.bfloat16)

    def across(t, d):
        return pltpu.make_async_remote_copy(
            src_ref=sib_term.at[d, t], dst_ref=sib_in.at[d, t],
            send_sem=sib_send.at[d, t], recv_sem=sib_recv.at[d, t],
            device_id={"dp": other}, device_id_type=MESH,
        )

    def terms(t):
        collect(t)
        for d in order:
            sib_term[d, t] = part(d, other, t)
            across(t, d).start()
        for d in order:
            term[d, t] = part(d, core, t)

    def hop(t, d, side):
        landing, arrival = (from_left, left_recv) if side > 0 else (from_right, right_recv)
        return pltpu.make_async_remote_copy(
            src_ref=term.at[d, t], dst_ref=landing.at[d, t],
            send_sem=hop_send.at[d, t], recv_sem=arrival.at[d, t],
            device_id={"seq": me + side}, device_id_type=MESH,
        )

    last = sources - 1

    def add(t, d, arrived):
        term[d, t] = (
            term[d, t].astype(jnp.float32) + arrived[d, t].astype(jnp.float32)
        ).astype(jnp.bfloat16)

    def hops(t):
        for d in order:
            across(t, d).wait_recv()
            add(t, d, sib_in)

            @pl.when(jnp.logical_and(me < d, me > 0))
            def _():
                hop(t, d, 1).wait_recv()
                add(t, d, from_left)

            @pl.when(jnp.logical_and(me > d, me < last))
            def _():
                hop(t, d, -1).wait_recv()
                add(t, d, from_right)

            @pl.when(me < d)
            def _():
                hop(t, d, 1).start()

            @pl.when(me > d)
            def _():
                hop(t, d, -1).start()

    def store(side, t):
        copy = pltpu.make_async_copy(
            total.at[side, t],
            weight_out.at[t, pl.ds(pl.multiple_of(side * half, half), half), :],
            store_sem.at[side, t],
        )
        copy.start()
        outs.append(copy)

    finals = {}

    def finish(t):
        total[core, t] = term[me, t].astype(jnp.float32)

        @pl.when(me > 0)
        def _():
            hop(t, me, 1).wait_recv()
            total[core, t] += from_left[me, t].astype(jnp.float32)

        @pl.when(me < last)
        def _():
            hop(t, me, -1).wait_recv()
            total[core, t] += from_right[me, t].astype(jnp.float32)

        finals[t] = remote(
            total.at[core, t], total.at[core, t], half_send.at[t], half_recv.at[t], {"dp": other}
        )
        store(core, t)

    terms(2)
    terms(0)
    hops(2)
    terms(1)
    hops(0)
    finish(2)
    hops(1)
    finish(0)
    for copy in cent_copies:
        copy.wait()
    sums = [cent_all[h, pl.ds(me, 1), :] for h in range(sources)]
    sums = jnp.concatenate(sums, axis=0)
    dirs_out[...] = sums * lax.rsqrt(jnp.mean(sums * sums, axis=-1, keepdims=True) + 1e-06)
    finish(1)
    for t in (2, 0, 1):
        for d in order:
            across(t, d).wait_send()

            @pl.when(me < d)
            def _():
                hop(t, d, 1).wait_send()

            @pl.when(me > d)
            def _():
                hop(t, d, -1).wait_send()

    for t in (2, 0, 1):
        finals[t].wait()
        store(other, t)
    for copy in outs:
        copy.wait()


def settle(*refs):
    count = (len(refs) - 1) // 3
    sem = refs[-1]
    came = [
        pltpu.make_async_copy(refs[i], refs[2 * count + i], sem.at[0, i]) for i in range(count)
    ]
    went = [
        pltpu.make_async_copy(refs[2 * count + i], refs[count + i], sem.at[1, i])
        for i in range(count)
    ]
    for copy in came:
        copy.start()
    for i in range(count):
        came[i].wait()
        went[i].start()
    for copy in went:
        copy.wait()


def by_head(layer_input, queries, keys, values, out_grad, cluster_ids, slots, counts):
    sources = lax.axis_size("seq")
    heads_here = cluster_ids.shape[1]
    tokens = queries.shape[1]
    width = queries.shape[2] // heads_here
    model = layer_input.shape[2]
    clusters = sources * counts.shape[2]
    every = sources * tokens
    half = model // sources // 2
    cols = heads_here * width
    chunk = 256
    low, wide = jnp.bfloat16, jnp.float32
    inside = pl.BlockSpec(memory_space=pltpu.VMEM)
    anywhere = pl.BlockSpec(memory_space=pl.ANY)
    dma = pltpu.SemaphoreType.DMA
    token_grad = jax.ShapeDtypeStruct((tokens, cols), low)
    results = pl.pallas_call(
        functools.partial(exchange, sources, tokens, width, model, clusters),
        out_shape=(
            token_grad, token_grad, token_grad,
            jax.ShapeDtypeStruct((3, model // sources, cols), wide),
            jax.ShapeDtypeStruct((heads_here, width), wide),
        ),
        in_specs=[anywhere] * 5 + [inside] * 2,
        out_specs=(anywhere,) * 4 + (inside,),
        scratch_shapes=[
            pltpu.VMEM((4, every, width), low),
            pltpu.VMEM((sources, 8, tokens), wide),
            pltpu.VMEM((sources, 8, tokens), wide),
            pltpu.VMEM((every, 2 * width), low),
            pltpu.VMEM((every, 2 * width), low),
            pltpu.VMEM((every, width), wide),
            pltpu.VMEM((every // chunk, every, chunk), wide),
            pltpu.VMEM((every, width), wide),
            pltpu.VMEM((3, every, width), low),
            pltpu.VMEM((3, tokens, cols), low),
            pltpu.VMEM((tokens, model), low),
            pltpu.VMEM((model, tokens), low),
            pltpu.VMEM((sources, 3, half, cols), low),
            pltpu.VMEM((sources, 3, half, cols), low),
            pltpu.VMEM((sources, 3, half, cols), low),
            pltpu.VMEM((sources, 3, half, cols), low),
            pltpu.VMEM((sources, 3, half, cols), low),
            pltpu.VMEM((2, 3, half, cols), wide),
            pltpu.VMEM((8, width), wide),
            pltpu.VMEM((8, width), wide),
            pltpu.VMEM((sources, 8, width), wide),
            dma((4, sources - 1)), dma((4, sources - 1)),
            dma((sources - 1,)), dma((sources - 1,)), dma((5,)),
            dma((3, sources - 1)), dma((3, sources - 1)),
            dma((sources, 3)), dma((sources, 3)),
            dma((sources, 3)), dma((sources, 3)), dma((sources, 3)),
            dma((3,)), dma((3,)),
            dma((sources,)), dma((sources,)), dma((4,)), dma((2, 3)),
        ],
        compiler_params=pltpu.CompilerParams(
            collective_id=0, has_side_effects=True, vmem_limit_bytes=60 * 1024 * 1024
        ),
    )(layer_input[0], queries[0], keys[0], values[0], out_grad[0], cluster_ids[0], slots[0])
    query_grad, key_grad, value_grad, weight, dirs = pl.pallas_call(
        settle,
        out_shape=tuple(jax.ShapeDtypeStruct(a.shape, a.dtype) for a in results),
        in_specs=[anywhere] * 5,
        out_specs=(anywhere,) * 5,
        scratch_shapes=[pltpu.VMEM(a.shape, a.dtype) for a in results] + [dma((2, 5))],
        compiler_params=pltpu.CompilerParams(vmem_limit_bytes=60 * 1024 * 1024),
    )(*results)
    return (
        query_grad[None], key_grad[None], value_grad[None],
        weight.transpose(1, 0, 2), dirs[:, None, :],
    )


def for_sending(value):
    return jax.tree.map(lambda a: a.astype(jnp.bfloat16) if a.dtype == jnp.float32 else a, value)


def contract_rows(left, right):
    return lax.dot_general(
        left, right, (((0,), (0,)), ((), ())), preferred_element_type=jnp.float32
    )


def contract_cols(left, right):
    return lax.dot_general(
        left, right, (((1,), (1,)), ((), ())), preferred_element_type=jnp.float32
    )


def unit_rows(array):
    wide = array.astype(jnp.float32)
    return wide * lax.rsqrt(jnp.mean(wide * wide, axis=-1, keepdims=True) + 1e-06)


def block_backward(block, live, rows):
    width = block.shape[1] // 4
    scale = width ** (-0.5)
    query = block[:, :width]
    key = block[:, width : 2 * width]
    value = block[:, 2 * width : 3 * width]
    grad = block[:, 3 * width :]
    key_total = jnp.zeros((block.shape[0], width), jnp.float32)
    value_total = jnp.zeros((block.shape[0], width), jnp.float32)
    query_parts = []
    for start in range(0, block.shape[0], rows):
        query_rows = query[start : start + rows]
        grad_rows = grad[start : start + rows]
        scores = contract_cols(query_rows, key) * scale
        scores = jnp.where(live[None, :], scores, -1e30)
        top = jnp.max(scores, axis=1, keepdims=True)
        weights = jnp.exp(scores - top)
        probs = weights / jnp.sum(weights, axis=1, keepdims=True)
        probs_low = probs.astype(jnp.bfloat16)
        recomputed = jnp.dot(probs_low, value, preferred_element_type=jnp.float32)
        delta = jnp.sum(grad_rows.astype(jnp.float32) * recomputed, axis=1, keepdims=True)
        dprobs = contract_cols(grad_rows, value)
        dscores = (probs * (dprobs - delta)).astype(jnp.bfloat16)
        query_parts.append(jnp.dot(dscores, key, preferred_element_type=jnp.float32) * scale)
        key_total = key_total + contract_rows(dscores, query_rows)
        value_total = value_total + contract_rows(probs_low, grad_rows)
    query_total = jnp.concatenate(query_parts, axis=0)
    return jnp.concatenate((query_total, key_total * scale, value_total), axis=1).astype(
        jnp.bfloat16
    )


def by_cluster(layer_input, queries, keys, values, out_grad, cluster_ids, slots, counts):
    sources = lax.axis_size("seq")
    heads_here = cluster_ids.shape[1]
    tokens_here = queries.shape[1]
    width = queries.shape[2] // heads_here
    clusters_here = counts.shape[2]
    reserved = CAP // sources
    block_rows = clusters_here * reserved
    total_rows = sources * block_rows

    def per_head(array):
        return array[0].reshape(tokens_here, heads_here, width).transpose(1, 0, 2)

    query_heads = per_head(queries)
    key_heads = per_head(keys)
    rows = jnp.concatenate((query_heads, key_heads, per_head(values), per_head(out_grad)), axis=2)
    cluster = cluster_ids[0]
    slot = slots[0]
    kept = slot >= 0
    place = jnp.where(kept, cluster * reserved + slot % reserved, total_rows)

    def fill(row_set, spots):
        return (
            jnp.zeros((total_rows + 1, row_set.shape[1]), row_set.dtype)
            .at[spots]
            .set(row_set)[:total_rows]
        )

    outgoing = jax.vmap(fill)(rows, place).reshape(heads_here, sources, block_rows, 4 * width)
    within = jnp.arange(reserved, dtype=jnp.int32)
    live = (within[None, None, None, :] < counts[0][..., None]).reshape(
        heads_here, clusters_here, CAP
    )
    arrived = lax.all_to_all(outgoing, "seq", split_axis=1, concat_axis=1, tiled=True)
    number = arrived.shape[0]
    blocks = arrived.reshape(number, sources, clusters_here, reserved, 4 * width)
    blocks = blocks.transpose(0, 2, 1, 3, 4).reshape(number * clusters_here, CAP, 4 * width)
    flat_mask = live.reshape(number * clusters_here, CAP)
    grads = lax.map(
        lambda item: block_backward(item[0], item[1], min(CAP, 512)), (blocks, flat_mask)
    )
    home = grads.reshape(number, clusters_here, sources, reserved, 3 * width)
    home = home.transpose(0, 2, 1, 3, 4).reshape(number, sources, block_rows, 3 * width)
    unit = (unit_rows(blocks[..., :width]) + unit_rows(blocks[..., width : 2 * width])) * flat_mask[
        ..., None
    ].astype(jnp.float32)
    sums = jnp.sum(unit, axis=1).reshape(number, clusters_here, width)
    home, owner_total = (home, sums)
    returned = lax.all_to_all(
        for_sending(home), "seq", split_axis=1, concat_axis=1, tiled=True
    ).astype(home.dtype)
    padded = jnp.concatenate(
        (
            returned.reshape(heads_here, total_rows, 3 * width),
            jnp.zeros((heads_here, 1, 3 * width), returned.dtype),
        ),
        axis=1,
    )
    back = jax.vmap(lambda table, spots: table[spots])(padded, place)

    def token_major(part):
        return part.transpose(1, 0, 2).reshape(tokens_here, heads_here * width)

    query_grad = token_major(back[:, :, :width])
    key_grad = token_major(back[:, :, width : 2 * width])
    value_grad = token_major(back[:, :, 2 * width :])
    stacked = jnp.stack((query_grad, key_grad, value_grad), axis=1).reshape(
        tokens_here, 3 * heads_here * width
    )
    inputs = layer_input[0]
    weight_share = lax.psum_scatter(
        contract_rows(inputs, stacked)
        .reshape(lax.axis_size("seq") * (inputs.shape[1] // sources), 3, heads_here * width)
        .astype(jnp.bfloat16),
        "seq",
        scatter_dimension=0,
        tiled=True,
    )
    unit = (unit_rows(query_heads) + unit_rows(key_heads)) * kept[..., None].astype(jnp.float32)
    member = (cluster[..., None] == jnp.arange(sources * clusters_here, dtype=jnp.int32)).astype(
        jnp.float32
    )
    term = jnp.einsum("htc,hte->hce", member, unit, precision=lax.Precision.HIGHEST)
    centroid_part = lax.psum_scatter(
        term.astype(jnp.bfloat16), "seq", scatter_dimension=1, tiled=True
    )
    weight_grad, centroid_total = (
        lax.psum(weight_share, "dp").astype(jnp.float32),
        lax.psum(centroid_part, "dp").astype(jnp.float32),
    )
    centroid_dirs = centroid_total * lax.rsqrt(
        jnp.mean(centroid_total * centroid_total, axis=-1, keepdims=True) + 1e-06
    )
    return (query_grad[None], key_grad[None], value_grad[None], weight_grad, centroid_dirs)


def on_device(*arrays):
    cluster_ids, counts = arrays[5], arrays[7]
    sources = lax.axis_size("seq")
    if cluster_ids.shape[1] == sources and counts.shape[2] == 1 and sources <= 8:
        return by_head(*arrays)
    return by_cluster(*arrays)


def solution(mesh):
    return jax.shard_map(
        on_device,
        mesh=mesh,
        in_specs=(
            P(("groups", "dp"), "seq", None),
            P(("groups", "dp"), "seq", "clus"),
            P(("groups", "dp"), "seq", "clus"),
            P(("groups", "dp"), "seq", "clus"),
            P(("groups", "dp"), "seq", "clus"),
            P(("groups", "dp"), "clus", "seq"),
            P(("groups", "dp"), "clus", "seq"),
            P(("groups", "dp"), "clus", "seq", None),
        ),
        out_specs=(
            P(("groups", "dp"), "seq", "clus"),
            P(("groups", "dp"), "seq", "clus"),
            P(("groups", "dp"), "seq", "clus"),
            P(("groups", "seq"), None, "clus"),
            P(("groups", "clus"), "seq", None),
        ),
        check_vma=False,
    )
```
